32 devices in a mesh: groups: 2 (over x), expert: 16 (over z, y, core).
Axes of the slice: x: 2, y: 2, z: 4, core: 2. Of those that a mesh axis runs over, the one named last changes fastest.
Arguments:
- tokens: bfloat16 [4096, 1664], P(('groups', 'expert')), parts along dimension 0, may hold values from -6 to 6
- gate_probs: float32 [4096, 2], P(('groups', 'expert')), parts along dimension 0, may hold values from 0.1 to 1
- expert_ids: int32 [4096, 2], P(('groups', 'expert')), parts along dimension 0, may hold values from 0 to 3, all different within a row; in each aligned block of 128 rows (0 to 127, 128 to 255, ...) at most 65 rows name the same one
- priority: int32 [4096], P(('groups', 'expert')), parts along dimension 0, may hold values from 0 to 2047, each once
- weight_in: bfloat16 [16, 1664, 1024], P('expert'), may hold values from -0.15625 to 0.15625
- weight_out: bfloat16 [16, 1024, 1664], P('expert'), may hold values from -0.09375 to 0.09375
Outputs:
- combined: bfloat16 [4096, 1664], P(('groups', 'expert')), parts along dimension 0
The draws below stay inside these ranges and needn't reach their ends.
There are 2 independent parts, one for each index of `groups`. The reference program is written for one: setup_inputs(seed, part) draws one part's arguments, and reference() takes and returns one part's arrays. A program takes and returns all parts, laid end to end along the dimension named above; an argument that names none is the same for every part. Nothing has to cross between parts.
Inputs may be any that keep to these rules, and one draw needn't show every extreme that they name: `expert_ids`: in the rows of one device no expert is named by more than 65 rows over both columns; some expert reaches 65 in some device's rows. `priority`: each value occurs once in a group.
All inputs are finite; a program needn't handle non-finite values.
Results may differ from the reference program's by a relative error of at most 0.0065.
Values may be sent and summed in bfloat16 or wider, within the bound.
A program may use at most 128 MiB of HBM per device.

```python
import math
import jax
import jax.numpy as jnp
import numpy as np
from jax import lax

D = 1664
HIDDEN_SIZE = 4096
SPLIT = 4
TOK_DEV = 128
EXPERTS = 4
HID_DEV = 1024
TOKENS = 2048
CAP = 1024
MOST = 65
N_EXPERT = 16


def block_scale(stream_key, extent, cuts, low, high):
    level = 1.0
    for axis_at, shards_of in cuts:
        steps = jax.random.uniform(jax.random.fold_in(jax.random.fold_in(stream_key, 6), axis_at), (shards_of,), jnp.float32, low / len(cuts), high / len(cuts))
        level = level * jnp.repeat(jnp.exp(steps), extent[axis_at] // shards_of).reshape((-1,) + (1,) * (len(extent) - 1 - axis_at))
    return level


def routed_block(key, own, number, rows, number_of, top, limit, lean):
    sequence = jax.random.permutation(key, number_of)
    heavy_load, common = shares(number_of, rows * top, limit, lean, True), shares(number_of, rows * top, limit, lean, False)
    places = jnp.arange(number_of)

    def named(lengths, turn):
        used = int((lengths > 0).sum())
        fixed = max(1, used // 4)
        moved = fixed + (places - fixed + turn * (used - fixed)) % max(1, number_of - fixed)
        return jnp.zeros((number_of,), jnp.int32).at[sequence[jnp.where(places < fixed, places, moved)]].set(jnp.asarray(lengths, jnp.int32))

    lengths = jnp.where(number % 4 == 0, named(heavy_load, number // 4), named(common, number - number // 4 - 1))
    mixed = jax.random.permutation(jax.random.fold_in(own, 3), number_of)
    giver, sink = mixed[0:number_of // 2 * 2:2], mixed[1:number_of // 2 * 2:2]
    margin = jnp.minimum(lengths[giver] - 1, limit - lengths[sink]) // 2
    margin = jnp.where((giver == sequence[0]) | (sink == sequence[0]) | (lengths[sink] == 0), 0, jnp.maximum(margin, 0))
    moved = jax.random.randint(jax.random.fold_in(own, 4), (number_of // 2,), 0, 1 << 20) % (margin + 1)
    lengths = lengths.at[giver].add(-moved).at[sink].add(moved)
    labels = jnp.searchsorted(jnp.cumsum(lengths), jnp.arange(rows * top), side="right").astype(jnp.int32)
    grid = labels.reshape(top, rows).T
    grid = grid[jax.random.permutation(jax.random.fold_in(own, 1), rows)]
    turn = jax.random.randint(jax.random.fold_in(own, 2), (rows, 1), 0, top)
    return jnp.take_along_axis(grid, (jnp.arange(top)[None, :] + turn) % top, axis=1)


def shares(count, total, most, lean, full):
    loads = [(1 << 20) // math.isqrt(grade ** lean) + 1 for grade in range(1, count + 1)]
    largest = most if full else min(most, max(-(-total // count), total * loads[0] // sum(loads)))
    least = 1 if total - largest >= count - 1 else 0
    holding, spare = [largest] + [least] * (count - 1), total - largest - least * (count - 1)
    while spare > 0:
        candidates = [i for i in range(1, count) if holding[i] < largest] or [i for i in range(1, count) if holding[i] < most]
        mass, left = sum([loads[i] for i in candidates]), spare
        for i in candidates:
            extra = min(most - holding[i], max(1, left * loads[i] // mass), spare)
            holding[i] = holding[i] + extra
            spare = spare - extra
    return np.array(holding)


def bell_draw(rng, extent, scale, bound, pieces=(), kind=jnp.bfloat16):
    drawn = scale * jax.random.normal(rng, extent, jnp.float32)
    if pieces:
        drawn = drawn * block_scale(rng, extent, pieces, -0.22, 0.18)
    return jnp.clip(drawn, -bound, bound).astype(kind)


def setup_inputs(seed: int = 0, part: int = 0) -> dict:
    seeds = jax.random.split(jax.random.key(seed), 7)
    part_splits = jax.random.split(jax.random.fold_in(seeds[6], part), 7)
    tokens = bell_draw(part_splits[0], (TOKENS, D), 1.0, 6.0, ((0, 16),))
    gate_probs = jnp.clip(jnp.exp(math.log(1.0) - 2.3025851 * jax.random.uniform(part_splits[1], (TOKENS, 2), jnp.float32) ** block_scale(part_splits[1], (TOKENS, 2), ((0, 16),), -0.2, 0.2)), 0.1, 1.0)
    expert_ids_keys = jax.random.split(jax.random.fold_in(part_splits[2], 1), TOKENS // TOK_DEV)
    expert_ids_turns = jax.random.permutation(jax.random.fold_in(part_splits[2], 3), TOKENS // TOK_DEV)
    expert_ids = jax.vmap(lambda own, number: routed_block(jax.random.fold_in(part_splits[2], 2), own, number, TOK_DEV, EXPERTS, 2, MOST, 2))(expert_ids_keys, expert_ids_turns).reshape((TOKENS, 2))
    priority = jax.random.permutation(part_splits[3], TOKENS).astype(jnp.int32)
    weight_in = bell_draw(seeds[4], (N_EXPERT, D, HID_DEV), D ** -0.5, 0.15625, ((0, 16),))
    weight_out = bell_draw(seeds[5], (N_EXPERT, HID_DEV, D), HIDDEN_SIZE ** -0.5, 0.09375, ((0, 16),))
    return dict(tokens=tokens, gate_probs=gate_probs, expert_ids=expert_ids, priority=priority, weight_in=weight_in, weight_out=weight_out)


def earlier_count(column, by_rank, priority):
    ordered = column[by_rank]
    one_hot = (ordered[:, None] == jnp.arange(EXPERTS, dtype=jnp.int32)[None, :]).astype(jnp.int32)
    ahead = jnp.sum((jnp.cumsum(one_hot, 0) - one_hot) * one_hot, 1)
    return ahead[priority]


def reference(tokens, gate_probs, expert_ids, priority, weight_in, weight_out):
    count_all = tokens.shape[0]
    first_ids = expert_ids[:, 0]
    second_ids = expert_ids[:, 1]
    by_rank = jnp.zeros((count_all,), jnp.int32).at[priority].set(jnp.arange(count_all, dtype=jnp.int32))
    before_first = earlier_count(first_ids, by_rank, priority)
    before_second = earlier_count(second_ids, by_rank, priority)
    totals = jnp.sum((first_ids[:, None] == jnp.arange(EXPERTS, dtype=jnp.int32)[None, :]).astype(jnp.int32), 0)
    fill = jnp.minimum(totals, CAP)
    slot_first = before_first
    slot_second = fill[second_ids] + before_second
    kept_first = slot_first < CAP
    kept_second = slot_second < CAP
    outside = EXPERTS * CAP
    index_first = jnp.where(kept_first, first_ids * CAP + slot_first, outside).astype(jnp.int32)
    index_second = jnp.where(kept_second, second_ids * CAP + slot_second, outside).astype(jnp.int32)
    buffer = jnp.zeros((EXPERTS * CAP, D), jnp.bfloat16)
    buffer = buffer.at[index_first].set(tokens, mode="drop")
    buffer = buffer.at[index_second].set(tokens, mode="drop")
    inner = weight_in.reshape(EXPERTS, SPLIT, D, HID_DEV)
    outer = weight_out.reshape(EXPERTS, SPLIT, HID_DEV, D)

    def serve_rows(operands):
        arrived, first_proj, second_proj = operands
        summed = jnp.zeros((arrived.shape[0], D), jnp.float32)
        for part_index in range(SPLIT):
            hidden = jax.nn.gelu(jnp.dot(arrived, first_proj[part_index], preferred_element_type=jnp.float32), approximate=False).astype(jnp.bfloat16)
            partial_value = jnp.dot(hidden, second_proj[part_index], preferred_element_type=jnp.float32).astype(jnp.bfloat16)
            partial_value = lax.optimization_barrier(partial_value)
            summed = summed + partial_value.astype(jnp.float32)
        return lax.optimization_barrier(summed.astype(jnp.bfloat16))

    outputs = lax.map(serve_rows, (buffer.reshape(EXPERTS, CAP, D), inner, outer)).reshape(EXPERTS * CAP, D)
    picked_first = outputs[jnp.minimum(index_first, outside - 1)].astype(jnp.float32)
    picked_second = outputs[jnp.minimum(index_second, outside - 1)].astype(jnp.float32)
    weight_first = jnp.where(kept_first, gate_probs[:, 0], jnp.float32(0.0))
    weight_second = jnp.where(kept_second, gate_probs[:, 1], jnp.float32(0.0))
    combined = weight_first[:, None] * picked_first + weight_second[:, None] * picked_second
    return combined.astype(jnp.bfloat16)
```

```python
import functools

import jax
import jax.numpy as jnp
from jax import lax
from jax.experimental import pallas as pl
from jax.experimental.pallas import tpu as pltpu
from jax.sharding import PartitionSpec as P

F32 = jnp.float32
BF16 = jnp.bfloat16


def gelu(x):
    return 0.5 * x * (1.0 + lax.erf(x * 0.7071067811865476))


def kernel(
    n_exp, base, tok, width,
    tokens, gates, ids, rank_col, meta, w_in, w_out,
    out,
    w1, w2, snd, rows, xs, hs, ext_in, ext_out, give, got, keep, ysend, ygot, rsend, ret, info, acc,
    w_sem, z_s, z_r, fs_s, fs_r, fy_s, fy_r, ff_s, ff_r, g_s, g_r, y_s, y_r, r_s, r_r,
    mz_s, mz_r, mp_s, mp_r,
):
    tiles = width // 128
    tail = tiles * base
    me = lax.axis_index("expert")
    plane, col = me // 4, me % 4
    sibling = plane * 4 + (col // 2) * 2 + (col + 1) % 2
    across = plane * 4 + (col + 2) % 4

    def peer(j):
        return ((plane + j) % n_exp) * 4 + col

    def remote(src, dst, send, recv, dev):
        return pltpu.make_async_remote_copy(
            src_ref=src, dst_ref=dst, send_sem=send, recv_sem=recv,
            device_id={"expert": dev}, device_id_type=pl.DeviceIdType.MESH,
        )

    def dispatch(j):
        return remote(snd.at[j], rows.at[0, j], z_s.at[j], z_r.at[j], peer(n_exp - j))

    def to_sibling(d):
        return remote(rows.at[0, d], rows.at[1, d], fs_s.at[d], fs_r.at[d], sibling)

    def to_across(d):
        return remote(rows.at[0, d], rows.at[2, d], fy_s.at[d], fy_r.at[d], across)

    def pass_on(d):
        return remote(rows.at[2, d], rows.at[3, d], ff_s.at[d], ff_r.at[d], sibling)

    def give_copy(d):
        return remote(give.at[d], got.at[d], g_s.at[d], g_r.at[d], sibling)

    def pair_copy(d):
        return remote(ysend.at[d], ygot.at[d], y_s.at[d], y_r.at[d], across)

    def return_copy(d):
        return remote(
            rsend.at[d], ret.at[n_exp - d], r_s.at[d], r_r.at[n_exp - d], peer(d)
        )

    def info_copy(j):
        return remote(info.at[0, 0], info.at[0, j], mz_s.at[j], mz_r.at[j], peer(n_exp - j))

    def info_sibling():
        return remote(info.at[0], info.at[1], mp_s.at[0], mp_r.at[0], sibling)

    def info_across():
        return remote(
            info.at[pl.ds(0, 2)], info.at[pl.ds(2, 2)], mp_s.at[1], mp_r.at[1], across
        )

    load_in = pltpu.make_async_copy(w_in.at[0], w1, w_sem.at[0])
    load_out = pltpu.make_async_copy(w_out.at[0], w2, w_sem.at[1])
    load_in.start()
    load_out.start()

    barrier = pltpu.get_barrier_semaphore()

    def greet(j, c):
        pl.semaphore_signal(
            barrier, inc=1, device_id={"expert": peer(j)}, device_id_type=pl.DeviceIdType.MESH
        )
        return c

    lax.fori_loop(1, n_exp, greet, 0)
    for dev in (sibling, across):
        pl.semaphore_signal(
            barrier, inc=1, device_id={"expert": dev}, device_id_type=pl.DeviceIdType.MESH
        )

    info[0, 0] = meta[...]
    ext_in[...] = jnp.zeros_like(ext_in)
    ext_out[...] = jnp.zeros_like(ext_out)
    first_row, second_row = meta[1:2, :], meta[2:3, :]
    upper = (
        lax.broadcasted_iota(jnp.int32, (tok, tok), 0)
        < lax.broadcasted_iota(jnp.int32, (tok, tok), 1)
    ).astype(BF16)
    slot_iota = lax.broadcasted_iota(jnp.int32, (base + 16, tok), 0).astype(F32)

    def pack(expert, dst):
        hit = ((first_row == expert) | (second_row == expert)).astype(F32)
        hit8 = jnp.broadcast_to(hit, (8, tok))
        place = jnp.dot(hit8.astype(BF16), upper, preferred_element_type=F32)[0:1, :]
        pick = jnp.where(slot_iota == place, hit, 0.0).astype(BF16)
        packed = jnp.dot(pick, tokens[...], preferred_element_type=F32)
        for c in range(tiles):
            lanes = slice(c * 128, (c + 1) * 128)
            dst[c * base : (c + 1) * base, :] = packed[:base, lanes].astype(BF16)
            ext_out[0, c : c + 1, :] = packed[base : base + 1, lanes]
        dst[tail : tail + 16, :] = ext_out[0].astype(BF16)

    pack(plane, rows.at[0, 0])
    pl.semaphore_wait(barrier, n_exp + 1)
    to_across(0).start()
    to_sibling(0).start()

    def start_info(j, c):
        info_copy(j).start()
        return c

    lax.fori_loop(1, n_exp, start_info, 0)

    def pack_send(j, c):
        pack((plane + n_exp - j) % n_exp, snd.at[j])
        dispatch(j).start()
        return c

    lax.fori_loop(1, n_exp, pack_send, 0)

    def wait_info(j, c):
        info_copy(j).wait_recv()
        return c

    lax.fori_loop(1, n_exp, wait_info, 0)
    info_sibling().start()
    info_sibling().wait_recv()
    info_across().start()
    load_in.wait()
    load_out.wait()

    order = (1, 3, 0, 2)

    def finish(d):
        pair_copy(d).wait_recv()
        rsend[d] = (keep[d, 0] + ygot[d].astype(F32)).astype(BF16)

    def group(d, c):
        @pl.when(d > 0)
        def _():
            dispatch(d).wait_recv()
            to_across(d).start()
            to_sibling(d).start()

        to_across(d).wait_recv()
        pass_on(d).start()
        to_sibling(d).wait_recv()
        pass_on(d).wait_recv()
        for i, rel in enumerate(order):
            last = rows[rel, d, tail : tail + 16, :].astype(F32)
            for t in range(tiles):
                lanes = slice(t * 128, (t + 1) * 128)
                xs[i * base : (i + 1) * base, lanes] = rows[rel, d, t * base : (t + 1) * base, :]
                ext_in[i : i + 1, lanes] = last[t : t + 1, :]
        xs[4 * base :, :] = ext_in[...].astype(BF16)
        hid = w1.shape[1]
        for n in range(0, hid, 256):
            h = jnp.dot(xs[...], w1[:, n : n + 256], preferred_element_type=F32)
            hs[:, n : n + 256] = gelu(h).astype(BF16)
        for n in range(0, width, 256):
            wide = min(256, width - n)
            p = jnp.dot(hs[...], w2[:, n : n + wide], preferred_element_type=F32)
            for t in range(n // 128, (n + wide) // 128):
                q = p[:, t * 128 - n : (t + 1) * 128 - n]
                span = slice(t * base, (t + 1) * base)
                give[d, 0, span, :] = q[:base].astype(BF16)
                give[d, 1, span, :] = q[base : 2 * base].astype(BF16)
                keep[d, 0, span, :] = q[2 * base : 3 * base]
                keep[d, 1, span, :] = q[3 * base : 4 * base]
                for i in range(4):
                    ext_out[i, t : t + 1, :] = q[4 * base + i : 4 * base + i + 1]
        for i in range(2):
            give[d, i, tail : tail + 16, :] = ext_out[i].astype(BF16)
            keep[d, i, tail : tail + 16, :] = ext_out[2 + i]
        give_copy(d).start()

        @pl.when(d > 0)
        def _():
            finish(d - 1)

        @pl.when(d > 1)
        def _():
            return_copy(d - 1).start()

        give_copy(d).wait_recv()
        ysend[d] = (keep[d, 1] + got[d, 1].astype(F32)).astype(BF16)
        pair_copy(d).start()
        keep[d, 0] = keep[d, 0] + got[d, 0].astype(F32)
        return c

    lax.fori_loop(0, n_exp, group, 0)

    info_across().wait_recv()
    mine, first, second = rank_col[...], ids[:, 0:1], ids[:, 1:2]

    def count(m, sums):
        r, k = m // n_exp, m % n_exp
        block = info[r, k]
        ahead = block[0:1, :] < mine
        one, two = block[1:2, :], block[2:3, :]
        a, b, c = sums
        a = a + jnp.where((one == first) & ahead, 1.0, 0.0)
        b = b + jnp.where(one == second, 1.0, 0.0)
        c = c + jnp.where((two == second) & ahead, 1.0, 0.0)
        return a, b, c

    zero = jnp.zeros((tok, tok), F32)
    sums = lax.fori_loop(0, 4 * n_exp, count, (zero, zero, zero))
    before_first, total_first, before_second = [jnp.sum(v, axis=1, keepdims=True) for v in sums]
    capacity = float(8 * tok)
    weight_first = jnp.where(before_first < capacity, gates[:, 0:1], 0.0)
    weight_second = jnp.where(
        jnp.minimum(total_first, capacity) + before_second < capacity, gates[:, 1:2], 0.0
    )
    lower = (
        lax.broadcasted_iota(jnp.int32, (tok, tok), 1)
        < lax.broadcasted_iota(jnp.int32, (tok, tok), 0)
    ).astype(BF16)
    lane = lax.broadcasted_iota(jnp.int32, (tok, tok), 1).astype(F32)

    def combine(expert, block):
        one, two = first == expert, second == expert
        hit = jnp.where(one | two, 1.0, 0.0)
        weight = jnp.where(one, weight_first, jnp.where(two, weight_second, 0.0))
        place = jnp.dot(
            lower, jnp.broadcast_to(hit, (tok, tok)).astype(BF16), preferred_element_type=F32
        )
        pick = jnp.where(place == lane, hit, 0.0).astype(BF16)[:, :base]
        over = jnp.where(place[:, 0:1] == float(base), weight, 0.0) * hit
        last = block[tail : tail + 16, :].astype(F32)
        values = jnp.concatenate(
            [block[t * base : (t + 1) * base, :] for t in range(tiles)], axis=1
        )
        found = jnp.dot(pick, values, preferred_element_type=F32)
        for t in range(tiles):
            lanes = slice(t * 128, (t + 1) * 128)
            acc[:, lanes] += weight * found[:, lanes] + over * last[t : t + 1, :]

    acc[...] = jnp.zeros_like(acc)
    combine(plane, rsend.at[0])
    finish(n_exp - 1)
    return_copy(n_exp - 1).start()

    def collect(i, c):
        j = n_exp - i
        return_copy(i).wait_recv()
        combine((plane + j) % n_exp, ret.at[j])
        return c

    lax.fori_loop(1, n_exp, collect, 0)
    out[...] = acc[...].astype(BF16)

    def drain(d, c):
        to_across(d).wait_send()
        to_sibling(d).wait_send()
        pass_on(d).wait_send()
        give_copy(d).wait_send()
        pair_copy(d).wait_send()

        @pl.when(d > 0)
        def _():
            dispatch(d).wait_send()
            info_copy(d).wait_send()
            return_copy(d).wait_send()

        return c

    lax.fori_loop(0, n_exp, drain, 0)
    info_sibling().wait_send()
    info_across().wait_send()


def shards(tokens, gate_probs, expert_ids, priority, weight_in, weight_out):
    tok, width = tokens.shape
    n_exp = lax.axis_size("expert") // 4
    base = 2 * tok // n_exp
    hid = weight_in.shape[2]
    block = (width // 128) * base + 16
    meta = jnp.concatenate(
        [priority[None, :], expert_ids.T, jnp.zeros((5, tok), jnp.int32)], axis=0
    )
    vmem = pl.BlockSpec(memory_space=pltpu.VMEM)
    hbm = pl.BlockSpec(memory_space=pl.ANY)
    group_rows = 4 * base + 16
    dma = pltpu.SemaphoreType.DMA
    return pl.pallas_call(
        functools.partial(kernel, n_exp, base, tok, width),
        out_shape=jax.ShapeDtypeStruct((tok, width), BF16),
        in_specs=[vmem, vmem, vmem, vmem, vmem, hbm, hbm],
        out_specs=vmem,
        scratch_shapes=[
            pltpu.VMEM((width, hid), BF16),
            pltpu.VMEM((hid, width), BF16),
            pltpu.VMEM((n_exp, block, 128), BF16),
            pltpu.VMEM((4, n_exp, block, 128), BF16),
            pltpu.VMEM((group_rows, width), BF16),
            pltpu.VMEM((group_rows, hid), BF16),
            pltpu.VMEM((16, width), F32),
            pltpu.VMEM((4, 16, 128), F32),
            pltpu.VMEM((n_exp, 2, block, 128), BF16),
            pltpu.VMEM((n_exp, 2, block, 128), BF16),
            pltpu.VMEM((n_exp, 2, block, 128), F32),
            pltpu.VMEM((n_exp, block, 128), BF16),
            pltpu.VMEM((n_exp, block, 128), BF16),
            pltpu.VMEM((n_exp, block, 128), BF16),
            pltpu.VMEM((n_exp, block, 128), BF16),
            pltpu.VMEM((4, n_exp, 8, tok), jnp.int32),
            pltpu.VMEM((tok, width), F32),
            dma((2,)),
        ]
        + [dma((n_exp,))] * 16
        + [dma((2,))] * 2,
        compiler_params=pltpu.CompilerParams(
            collective_id=0, has_side_effects=True, vmem_limit_bytes=56 * 1024 * 1024
        ),
        cost_estimate=pl.CostEstimate(
            flops=4 * 8 * tok * width * hid,
            bytes_accessed=4 * width * hid,
            transcendentals=8 * tok * hid,
        ),
    )(tokens, gate_probs, expert_ids, priority[:, None], meta, weight_in, weight_out)


def solution(mesh):
    placed = (
        P(("groups", "expert"), None),
        P(("groups", "expert"), None),
        P(("groups", "expert"), None),
        P(("groups", "expert")),
        P("expert", None, None),
        P("expert", None, None),
    )
    return jax.shard_map(
        shards, mesh=mesh, in_specs=placed, out_specs=P(("groups", "expert"), None), check_vma=False
    )
```

```python
import functools

import jax
import jax.numpy as jnp
from jax import lax
from jax.experimental import pallas as pl
from jax.experimental.pallas import tpu as pltpu
from jax.sharding import PartitionSpec as P

F32 = jnp.float32
BF16 = jnp.bfloat16


def gelu(x):
    return 0.5 * x * (1.0 + lax.erf(x * 0.7071067811865476))


def kernel(
    n_exp, base, tok, width,
    tokens, gates, ids, rank, w_in, w_out,
    out,
    w1, w2, snd, rows, xs, hs, ext_in, ext_out, give, got, keep, ysend, ygot, rsend, ret, info, acc,
    w_sem, z_s, z_r, fs_s, fs_r, fy_s, fy_r, ff_s, ff_r, g_s, g_r, y_s, y_r, r_s, r_r,
    mz_s, mz_r, mp_s, mp_r,
):
    tiles = width // 128
    tail = tiles * base
    me = lax.axis_index("expert")
    plane, col = me // 4, me % 4
    sibling = plane * 4 + (col // 2) * 2 + (col + 1) % 2
    across = plane * 4 + (col + 2) % 4

    def peer(j):
        return ((plane + j) % n_exp) * 4 + col

    def remote(src, dst, send, recv, dev):
        return pltpu.make_async_remote_copy(
            src_ref=src, dst_ref=dst, send_sem=send, recv_sem=recv,
            device_id={"expert": dev}, device_id_type=pl.DeviceIdType.MESH,
        )

    def dispatch(j):
        return remote(snd.at[j], rows.at[0, j], z_s.at[j], z_r.at[j], peer(n_exp - j))

    def to_sibling(d):
        return remote(rows.at[0, d], rows.at[1, d], fs_s.at[d], fs_r.at[d], sibling)

    def to_across(d):
        return remote(rows.at[0, d], rows.at[2, d], fy_s.at[d], fy_r.at[d], across)

    def pass_on(d):
        return remote(rows.at[2, d], rows.at[3, d], ff_s.at[d], ff_r.at[d], sibling)

    def give_copy(d):
        return remote(give.at[d], got.at[d], g_s.at[d], g_r.at[d], sibling)

    def pair_copy(d):
        return remote(ysend.at[d], ygot.at[d], y_s.at[d], y_r.at[d], across)

    def return_copy(d):
        return remote(
            rsend.at[d], ret.at[n_exp - d], r_s.at[d], r_r.at[n_exp - d], peer(d)
        )

    def info_copy(j):
        return remote(info.at[0, 0], info.at[0, j], mz_s.at[j], mz_r.at[j], peer(n_exp - j))

    def info_sibling():
        return remote(info.at[0], info.at[1], mp_s.at[0], mp_r.at[0], sibling)

    def info_across():
        return remote(
            info.at[pl.ds(0, 2)], info.at[pl.ds(2, 2)], mp_s.at[1], mp_r.at[1], across
        )

    load_in = pltpu.make_async_copy(w_in.at[0], w1, w_sem.at[0])
    load_out = pltpu.make_async_copy(w_out.at[0], w2, w_sem.at[1])
    load_in.start()
    load_out.start()

    barrier = pltpu.get_barrier_semaphore()

    def greet(j, c):
        pl.semaphore_signal(
            barrier, inc=1, device_id={"expert": peer(j)}, device_id_type=pl.DeviceIdType.MESH
        )
        return c

    lax.fori_loop(1, n_exp, greet, 0)
    for dev in (sibling, across):
        pl.semaphore_signal(
            barrier, inc=1, device_id={"expert": dev}, device_id_type=pl.DeviceIdType.MESH
        )

    info[0, 0] = jnp.concatenate(
        [rank[...].astype(F32), ids[...].astype(F32), gates[...], jnp.zeros((3, tok), F32)], axis=0
    )
    ext_in[...] = jnp.zeros_like(ext_in)
    ext_out[...] = jnp.zeros_like(ext_out)
    first_row, second_row = ids[0:1, :], ids[1:2, :]
    upper = (
        lax.broadcasted_iota(jnp.int32, (tok, tok), 0)
        < lax.broadcasted_iota(jnp.int32, (tok, tok), 1)
    ).astype(BF16)
    slot_iota = lax.broadcasted_iota(jnp.int32, (base + 16, tok), 0).astype(F32)

    def pack(expert, dst):
        hit = ((first_row == expert) | (second_row == expert)).astype(F32)
        hit8 = jnp.broadcast_to(hit, (8, tok))
        place = jnp.dot(hit8.astype(BF16), upper, preferred_element_type=F32)[0:1, :]
        pick = jnp.where(slot_iota == place, hit, 0.0).astype(BF16)
        packed = jnp.dot(pick, tokens[...], preferred_element_type=F32)
        for c in range(tiles):
            lanes = slice(c * 128, (c + 1) * 128)
            dst[c * base : (c + 1) * base, :] = packed[:base, lanes].astype(BF16)
            ext_out[0, c : c + 1, :] = packed[base : base + 1, lanes]
        dst[tail : tail + 16, :] = ext_out[0].astype(BF16)

    pack(plane, rows.at[0, 0])
    pl.semaphore_wait(barrier, n_exp + 1)
    to_across(0).start()
    to_sibling(0).start()

    def start_info(j, c):
        info_copy(j).start()
        return c

    lax.fori_loop(1, n_exp, start_info, 0)

    def pack_send(j, c):
        pack((plane + n_exp - j) % n_exp, snd.at[j])

        @pl.when(j == 1)
        def _():
            dispatch(j).start()

        return c

    lax.fori_loop(1, n_exp, pack_send, 0)

    def wait_info(j, c):
        info_copy(j).wait_recv()
        return c

    lax.fori_loop(1, n_exp, wait_info, 0)
    info_sibling().start()
    info_sibling().wait_recv()
    info_across().start()
    load_in.wait()
    load_out.wait()

    order = (1, 3, 0, 2)

    def finish(d):
        pair_copy(d).wait_recv()
        rsend[d] = (keep[d, 0] + ygot[d].astype(F32)).astype(BF16)

    def group(d, c):
        to_across(d).wait_recv()
        pass_on(d).start()

        @pl.when(d < n_exp - 1)
        def _():
            dispatch(d + 1).wait_send()

            @pl.when(d < n_exp - 2)
            def _():
                dispatch(d + 2).start()

            dispatch(d + 1).wait_recv()
            to_across(d + 1).start()
            to_sibling(d + 1).start()

        to_sibling(d).wait_recv()
        pass_on(d).wait_recv()
        for i, rel in enumerate(order):
            last = rows[rel, d, tail : tail + 16, :].astype(F32)
            for t in range(tiles):
                lanes = slice(t * 128, (t + 1) * 128)
                xs[i * base : (i + 1) * base, lanes] = rows[rel, d, t * base : (t + 1) * base, :]
                ext_in[i : i + 1, lanes] = last[t : t + 1, :]
        xs[4 * base :, :] = ext_in[...].astype(BF16)
        hid = w1.shape[1]
        for n in range(0, hid, 256):
            h = jnp.dot(xs[...], w1[:, n : n + 256], preferred_element_type=F32)
            hs[:, n : n + 256] = gelu(h).astype(BF16)
        for n in range(0, width, 256):
            wide = min(256, width - n)
            p = jnp.dot(hs[...], w2[:, n : n + wide], preferred_element_type=F32)
            for t in range(n // 128, (n + wide) // 128):
                q = p[:, t * 128 - n : (t + 1) * 128 - n]
                span = slice(t * base, (t + 1) * base)
                give[d, 0, span, :] = q[:base].astype(BF16)
                give[d, 1, span, :] = q[base : 2 * base].astype(BF16)
                keep[d, 0, span, :] = q[2 * base : 3 * base]
                keep[d, 1, span, :] = q[3 * base : 4 * base]
                for i in range(4):
                    ext_out[i, t : t + 1, :] = q[4 * base + i : 4 * base + i + 1]
        for i in range(2):
            give[d, i, tail : tail + 16, :] = ext_out[i].astype(BF16)
            keep[d, i, tail : tail + 16, :] = ext_out[2 + i]
        give_copy(d).start()

        @pl.when(d > 0)
        def _():
            finish(d - 1)

        @pl.when(d > 1)
        def _():
            return_copy(d - 1).start()

        give_copy(d).wait_recv()
        ysend[d] = (keep[d, 1] + got[d, 1].astype(F32)).astype(BF16)
        pair_copy(d).start()
        keep[d, 0] = keep[d, 0] + got[d, 0].astype(F32)
        return c

    lax.fori_loop(0, n_exp, group, 0)

    info_across().wait_recv()
    own = jnp.transpose(jnp.concatenate([info[0, 0]] * (tok // 8), axis=0))
    mine, first, second = own[:, 0:1], own[:, 1:2], own[:, 2:3]

    def count(m, sums):
        r, k = m // n_exp, m % n_exp
        block = info[r, k]
        ahead = block[0:1, :] < mine
        one, two = block[1:2, :], block[2:3, :]
        a, b, c = sums
        a = a + jnp.where((one == first) & ahead, 1.0, 0.0)
        b = b + jnp.where(one == second, 1.0, 0.0)
        c = c + jnp.where((two == second) & ahead, 1.0, 0.0)
        return a, b, c

    zero = jnp.zeros((tok, tok), F32)
    sums = lax.fori_loop(0, 4 * n_exp, count, (zero, zero, zero))
    before_first, total_first, before_second = [jnp.sum(v, axis=1, keepdims=True) for v in sums]
    capacity = float(8 * tok)
    weight_first = jnp.where(before_first < capacity, own[:, 3:4], 0.0)
    weight_second = jnp.where(
        jnp.minimum(total_first, capacity) + before_second < capacity, own[:, 4:5], 0.0
    )
    lower = (
        lax.broadcasted_iota(jnp.int32, (tok, tok), 1)
        < lax.broadcasted_iota(jnp.int32, (tok, tok), 0)
    ).astype(BF16)
    lane = lax.broadcasted_iota(jnp.int32, (tok, tok), 1).astype(F32)

    def combine(expert, block):
        named = expert.astype(F32)
        one, two = first == named, second == named
        hit = jnp.where(one | two, 1.0, 0.0)
        weight = jnp.where(one, weight_first, jnp.where(two, weight_second, 0.0))
        place = jnp.dot(
            lower, jnp.broadcast_to(hit, (tok, tok)).astype(BF16), preferred_element_type=F32
        )
        pick = jnp.where(place == lane, hit, 0.0).astype(BF16)[:, :base]
        over = jnp.where(place[:, 0:1] == float(base), weight, 0.0) * hit
        last = block[tail : tail + 16, :].astype(F32)
        values = jnp.concatenate(
            [block[t * base : (t + 1) * base, :] for t in range(tiles)], axis=1
        )
        found = jnp.dot(pick, values, preferred_element_type=F32)
        for t in range(tiles):
            lanes = slice(t * 128, (t + 1) * 128)
            acc[:, lanes] += weight * found[:, lanes] + over * last[t : t + 1, :]

    acc[...] = jnp.zeros_like(acc)
    combine(plane, rsend.at[0])
    finish(n_exp - 1)
    return_copy(n_exp - 1).start()

    def collect(i, c):
        j = n_exp - i
        return_copy(i).wait_recv()
        combine((plane + j) % n_exp, ret.at[j])
        return c

    lax.fori_loop(1, n_exp, collect, 0)
    out[...] = acc[...].astype(BF16)

    def drain(d, c):
        to_across(d).wait_send()
        to_sibling(d).wait_send()
        pass_on(d).wait_send()
        give_copy(d).wait_send()
        pair_copy(d).wait_send()

        @pl.when(d > 0)
        def _():
            info_copy(d).wait_send()
            return_copy(d).wait_send()

        return c

    lax.fori_loop(0, n_exp, drain, 0)
    info_sibling().wait_send()
    info_across().wait_send()


def shards(tokens, gate_probs, expert_ids, priority, weight_in, weight_out):
    tok, width = tokens.shape
    n_exp = lax.axis_size("expert") // 4
    base = 2 * tok // n_exp
    hid = weight_in.shape[2]
    block = (width // 128) * base + 16
    vmem = pl.BlockSpec(memory_space=pltpu.VMEM)
    hbm = pl.BlockSpec(memory_space=pl.ANY)
    group_rows = 4 * base + 16
    dma = pltpu.SemaphoreType.DMA
    return pl.pallas_call(
        functools.partial(kernel, n_exp, base, tok, width),
        out_shape=jax.ShapeDtypeStruct((tok, width), BF16),
        in_specs=[vmem, vmem, vmem, vmem, hbm, hbm],
        out_specs=vmem,
        scratch_shapes=[
            pltpu.VMEM((width, hid), BF16),
            pltpu.VMEM((hid, width), BF16),
            pltpu.VMEM((n_exp, block, 128), BF16),
            pltpu.VMEM((4, n_exp, block, 128), BF16),
            pltpu.VMEM((group_rows, width), BF16),
            pltpu.VMEM((group_rows, hid), BF16),
            pltpu.VMEM((16, width), F32),
            pltpu.VMEM((4, 16, 128), F32),
            pltpu.VMEM((n_exp, 2, block, 128), BF16),
            pltpu.VMEM((n_exp, 2, block, 128), BF16),
            pltpu.VMEM((n_exp, 2, block, 128), F32),
            pltpu.VMEM((n_exp, block, 128), BF16),
            pltpu.VMEM((n_exp, block, 128), BF16),
            pltpu.VMEM((n_exp, block, 128), BF16),
            pltpu.VMEM((n_exp, block, 128), BF16),
            pltpu.VMEM((4, n_exp, 8, tok), F32),
            pltpu.VMEM((tok, width), F32),
            dma((2,)),
        ]
        + [dma((n_exp,))] * 16
        + [dma((2,))] * 2,
        compiler_params=pltpu.CompilerParams(
            collective_id=0, has_side_effects=True, vmem_limit_bytes=56 * 1024 * 1024
        ),
        cost_estimate=pl.CostEstimate(
            flops=4 * 8 * tok * width * hid,
            bytes_accessed=4 * width * hid,
            transcendentals=8 * tok * hid,
        ),
    )(tokens, gate_probs.T, expert_ids.T, priority[None, :], weight_in, weight_out)


def solution(mesh):
    placed = (
        P(("groups", "expert"), None),
        P(("groups", "expert"), None),
        P(("groups", "expert"), None),
        P(("groups", "expert")),
        P("expert", None, None),
        P("expert", None, None),
    )
    return jax.shard_map(
        shards, mesh=mesh, in_specs=placed, out_specs=P(("groups", "expert"), None), check_vma=False
    )
```

```python
import functools

import jax
import jax.numpy as jnp
from jax import lax
from jax.experimental import pallas as pl
from jax.experimental.pallas import tpu as pltpu
from jax.sharding import PartitionSpec as P

F32 = jnp.float32
BF16 = jnp.bfloat16


def gelu(x):
    return 0.5 * x * (1.0 + lax.erf(x * 0.7071067811865476))


def kernel(
    n_exp, base, tok, width,
    tokens, gates, ids, rank, w_in, w_out,
    out,
    w1, w2, snd, rows, xs, hs, ext_in, ext_out, give, got, keep, ysend, ygot, rsend, ret, info, acc,
    w_sem, z_s, z_r, fs_s, fs_r, fy_s, fy_r, ff_s, ff_r, g_s, g_r, y_s, y_r, r_s, r_r,
    mz_s, mz_r, mp_s, mp_r,
):
    tiles = width // 128
    tail = tiles * base
    cut = tail // 32 * 16
    halves = ((0, cut), (cut, tail + 16 - cut))
    me = lax.axis_index("expert")
    plane, col = me // 4, me % 4
    sibling = plane * 4 + (col // 2) * 2 + (col + 1) % 2
    across = plane * 4 + (col + 2) % 4

    def peer(j):
        return ((plane + j) % n_exp) * 4 + col

    def remote(src, dst, send, recv, dev):
        return pltpu.make_async_remote_copy(
            src_ref=src, dst_ref=dst, send_sem=send, recv_sem=recv,
            device_id={"expert": dev}, device_id_type=pl.DeviceIdType.MESH,
        )

    def dispatch(j):
        return remote(snd.at[j], rows.at[0, j], z_s.at[j], z_r.at[j], peer(n_exp - j))

    def to_sibling(d):
        return remote(rows.at[0, d], rows.at[1, d], fs_s.at[d], fs_r.at[d], sibling)

    def to_across(d):
        return remote(rows.at[0, d], rows.at[2, d], fy_s.at[d], fy_r.at[d], across)

    def pass_on(d):
        return remote(rows.at[2, d], rows.at[3, d], ff_s.at[d], ff_r.at[d], sibling)

    def give_copy(d):
        return remote(give.at[d], got.at[d], g_s.at[d], g_r.at[d], sibling)

    def pair_copy(d, h):
        span = pl.ds(*halves[h])
        return remote(
            ysend.at[d, span], ygot.at[d, span], y_s.at[2 * d + h], y_r.at[2 * d + h], across
        )

    def return_copy(d, h):
        span, j = pl.ds(*halves[h]), n_exp - d
        return remote(
            rsend.at[d, span], ret.at[j, span], r_s.at[2 * d + h], r_r.at[2 * j + h], peer(d)
        )

    def info_copy(j):
        return remote(info.at[0, 0], info.at[0, j], mz_s.at[j], mz_r.at[j], peer(n_exp - j))

    def info_sibling():
        return remote(info.at[0], info.at[1], mp_s.at[0], mp_r.at[0], sibling)

    def info_across():
        return remote(
            info.at[pl.ds(0, 2)], info.at[pl.ds(2, 2)], mp_s.at[1], mp_r.at[1], across
        )

    load_in = pltpu.make_async_copy(w_in.at[0], w1, w_sem.at[0])
    load_out = pltpu.make_async_copy(w_out.at[0], w2, w_sem.at[1])
    load_in.start()
    load_out.start()

    barrier = pltpu.get_barrier_semaphore()

    def greet(j, c):
        pl.semaphore_signal(
            barrier, inc=1, device_id={"expert": peer(j)}, device_id_type=pl.DeviceIdType.MESH
        )
        return c

    lax.fori_loop(1, n_exp, greet, 0)
    for dev in (sibling, across):
        pl.semaphore_signal(
            barrier, inc=1, device_id={"expert": dev}, device_id_type=pl.DeviceIdType.MESH
        )

    info[0, 0] = jnp.concatenate(
        [rank[...].astype(F32), ids[...].astype(F32), gates[...], jnp.zeros((3, tok), F32)], axis=0
    )
    ext_in[...] = jnp.zeros_like(ext_in)
    ext_out[...] = jnp.zeros_like(ext_out)
    first_row, second_row = ids[0:1, :], ids[1:2, :]
    upper = (
        lax.broadcasted_iota(jnp.int32, (tok, tok), 0)
        < lax.broadcasted_iota(jnp.int32, (tok, tok), 1)
    ).astype(BF16)
    slot_iota = lax.broadcasted_iota(jnp.int32, (base + 16, tok), 0).astype(F32)

    def pack(expert, dst):
        hit = ((first_row == expert) | (second_row == expert)).astype(F32)
        hit8 = jnp.broadcast_to(hit, (8, tok))
        place = jnp.dot(hit8.astype(BF16), upper, preferred_element_type=F32)[0:1, :]
        pick = jnp.where(slot_iota == place, hit, 0.0).astype(BF16)
        packed = jnp.dot(pick, tokens[...], preferred_element_type=F32)
        for c in range(tiles):
            lanes = slice(c * 128, (c + 1) * 128)
            dst[c * base : (c + 1) * base, :] = packed[:base, lanes].astype(BF16)
            ext_out[0, c : c + 1, :] = packed[base : base + 1, lanes]
        dst[tail : tail + 16, :] = ext_out[0].astype(BF16)

    pack(plane, rows.at[0, 0])
    pl.semaphore_wait(barrier, n_exp + 1)
    to_across(0).start()
    to_sibling(0).start()

    def start_info(j, c):
        info_copy(j).start()
        return c

    lax.fori_loop(1, n_exp, start_info, 0)

    def pack_send(j, c):
        pack((plane + n_exp - j) % n_exp, snd.at[j])

        @pl.when(j == 1)
        def _():
            dispatch(j).start()

        return c

    lax.fori_loop(1, n_exp, pack_send, 0)

    def wait_info(j, c):
        info_copy(j).wait_recv()
        return c

    lax.fori_loop(1, n_exp, wait_info, 0)
    info_sibling().start()
    info_sibling().wait_recv()
    info_across().start()
    load_in.wait()
    load_out.wait()

    order = (1, 3, 0, 2)

    def finish(d, h):
        span = pl.ds(*halves[h])
        pair_copy(d, h).wait_recv()
        rsend[d, span] = (keep[d, 0, span] + ygot[d, span].astype(F32)).astype(BF16)

    def add_pair(d, h):
        span = pl.ds(*halves[h])
        ysend[d, span] = (keep[d, 1, span] + got[d, 1, span].astype(F32)).astype(BF16)
        pair_copy(d, h).start()

    def group(d, c):
        to_across(d).wait_recv()
        pass_on(d).start()

        @pl.when(d < n_exp - 1)
        def _():
            dispatch(d + 1).wait_send()

            @pl.when(d < n_exp - 2)
            def _():
                dispatch(d + 2).start()

            dispatch(d + 1).wait_recv()
            to_across(d + 1).start()
            to_sibling(d + 1).start()

        to_sibling(d).wait_recv()
        pass_on(d).wait_recv()
        for i, rel in enumerate(order):
            last = rows[rel, d, tail : tail + 16, :].astype(F32)
            for t in range(tiles):
                lanes = slice(t * 128, (t + 1) * 128)
                xs[i * base : (i + 1) * base, lanes] = rows[rel, d, t * base : (t + 1) * base, :]
                ext_in[i : i + 1, lanes] = last[t : t + 1, :]
        xs[4 * base :, :] = ext_in[...].astype(BF16)
        hid = w1.shape[1]
        for n in range(0, hid, 256):
            h = jnp.dot(xs[...], w1[:, n : n + 256], preferred_element_type=F32)
            hs[:, n : n + 256] = gelu(h).astype(BF16)
        for n in range(0, width, 256):
            wide = min(256, width - n)
            p = jnp.dot(hs[...], w2[:, n : n + wide], preferred_element_type=F32)
            for t in range(n // 128, (n + wide) // 128):
                q = p[:, t * 128 - n : (t + 1) * 128 - n]
                span = slice(t * base, (t + 1) * base)
                give[d, 0, span, :] = q[:base].astype(BF16)
                give[d, 1, span, :] = q[base : 2 * base].astype(BF16)
                keep[d, 0, span, :] = q[2 * base : 3 * base]
                keep[d, 1, span, :] = q[3 * base : 4 * base]
                for i in range(4):
                    ext_out[i, t : t + 1, :] = q[4 * base + i : 4 * base + i + 1]
        for i in range(2):
            give[d, i, tail : tail + 16, :] = ext_out[i].astype(BF16)
            keep[d, i, tail : tail + 16, :] = ext_out[2 + i]
        give_copy(d).start()

        @pl.when(d > 0)
        def _():
            finish(d - 1, 0)
            finish(d - 1, 1)

        @pl.when(d > 1)
        def _():
            return_copy(d - 1, 0).start()
            return_copy(d - 1, 1).start()

        give_copy(d).wait_recv()
        add_pair(d, 0)

        @pl.when(d < n_exp - 1)
        def _():
            add_pair(d, 1)

        keep[d, 0] = keep[d, 0] + got[d, 0].astype(F32)
        return c

    lax.fori_loop(0, n_exp, group, 0)

    info_across().wait_recv()
    own = jnp.transpose(jnp.concatenate([info[0, 0]] * (tok // 8), axis=0))
    mine, first, second = own[:, 0:1], own[:, 1:2], own[:, 2:3]

    def count(m, sums):
        r, k = m // n_exp, m % n_exp
        block = info[r, k]
        ahead = block[0:1, :] < mine
        one, two = block[1:2, :], block[2:3, :]
        a, b, c = sums
        a = a + jnp.where((one == first) & ahead, 1.0, 0.0)
        b = b + jnp.where(one == second, 1.0, 0.0)
        c = c + jnp.where((two == second) & ahead, 1.0, 0.0)
        return a, b, c

    zero = jnp.zeros((tok, tok), F32)
    sums = lax.fori_loop(0, 4 * n_exp, count, (zero, zero, zero))
    before_first, total_first, before_second = [jnp.sum(v, axis=1, keepdims=True) for v in sums]
    capacity = float(8 * tok)
    weight_first = jnp.where(before_first < capacity, own[:, 3:4], 0.0)
    weight_second = jnp.where(
        jnp.minimum(total_first, capacity) + before_second < capacity, own[:, 4:5], 0.0
    )
    lower = (
        lax.broadcasted_iota(jnp.int32, (tok, tok), 1)
        < lax.broadcasted_iota(jnp.int32, (tok, tok), 0)
    ).astype(BF16)
    lane = lax.broadcasted_iota(jnp.int32, (tok, tok), 1).astype(F32)

    def combine(expert, block):
        named = expert.astype(F32)
        one, two = first == named, second == named
        hit = jnp.where(one | two, 1.0, 0.0)
        weight = jnp.where(one, weight_first, jnp.where(two, weight_second, 0.0))
        place = jnp.dot(
            lower, jnp.broadcast_to(hit, (tok, tok)).astype(BF16), preferred_element_type=F32
        )
        pick = jnp.where(place == lane, hit, 0.0).astype(BF16)[:, :base]
        over = jnp.where(place[:, 0:1] == float(base), weight, 0.0) * hit
        last = block[tail : tail + 16, :].astype(F32)
        values = jnp.concatenate(
            [block[t * base : (t + 1) * base, :] for t in range(tiles)], axis=1
        )
        found = jnp.dot(pick, values, preferred_element_type=F32)
        for t in range(tiles):
            lanes = slice(t * 128, (t + 1) * 128)
            acc[:, lanes] += weight * found[:, lanes] + over * last[t : t + 1, :]

    acc[...] = jnp.zeros_like(acc)
    pair_copy(n_exp - 1, 0).wait_send()
    add_pair(n_exp - 1, 1)
    finish(n_exp - 1, 0)
    return_copy(n_exp - 1, 0).start()
    combine(plane, rsend.at[0])
    finish(n_exp - 1, 1)
    return_copy(n_exp - 1, 1).start()

    def collect(i, c):
        j = n_exp - i
        return_copy(i, 0).wait_recv()
        return_copy(i, 1).wait_recv()
        combine((plane + j) % n_exp, ret.at[j])
        return c

    lax.fori_loop(1, n_exp, collect, 0)
    out[...] = acc[...].astype(BF16)

    def drain(d, c):
        to_across(d).wait_send()
        to_sibling(d).wait_send()
        pass_on(d).wait_send()
        give_copy(d).wait_send()
        pair_copy(d, 1).wait_send()

        @pl.when(d < n_exp - 1)
        def _():
            pair_copy(d, 0).wait_send()

        @pl.when(d > 0)
        def _():
            info_copy(d).wait_send()
            return_copy(d, 0).wait_send()
            return_copy(d, 1).wait_send()

        return c

    lax.fori_loop(0, n_exp, drain, 0)
    info_sibling().wait_send()
    info_across().wait_send()


def shards(tokens, gate_probs, expert_ids, priority, weight_in, weight_out):
    tok, width = tokens.shape
    n_exp = lax.axis_size("expert") // 4
    base = 2 * tok // n_exp
    hid = weight_in.shape[2]
    block = (width // 128) * base + 16
    vmem = pl.BlockSpec(memory_space=pltpu.VMEM)
    hbm = pl.BlockSpec(memory_space=pl.ANY)
    group_rows = 4 * base + 16
    dma = pltpu.SemaphoreType.DMA
    return pl.pallas_call(
        functools.partial(kernel, n_exp, base, tok, width),
        out_shape=jax.ShapeDtypeStruct((tok, width), BF16),
        in_specs=[vmem, vmem, vmem, vmem, hbm, hbm],
        out_specs=vmem,
        scratch_shapes=[
            pltpu.VMEM((width, hid), BF16),
            pltpu.VMEM((hid, width), BF16),
            pltpu.VMEM((n_exp, block, 128), BF16),
            pltpu.VMEM((4, n_exp, block, 128), BF16),
            pltpu.VMEM((group_rows, width), BF16),
            pltpu.VMEM((group_rows, hid), BF16),
            pltpu.VMEM((16, width), F32),
            pltpu.VMEM((4, 16, 128), F32),
            pltpu.VMEM((n_exp, 2, block, 128), BF16),
            pltpu.VMEM((n_exp, 2, block, 128), BF16),
            pltpu.VMEM((n_exp, 2, block, 128), F32),
            pltpu.VMEM((n_exp, block, 128), BF16),
            pltpu.VMEM((n_exp, block, 128), BF16),
            pltpu.VMEM((n_exp, block, 128), BF16),
            pltpu.VMEM((n_exp, block, 128), BF16),
            pltpu.VMEM((4, n_exp, 8, tok), F32),
            pltpu.VMEM((tok, width), F32),
            dma((2,)),
        ]
        + [dma((n_exp,))] * 10
        + [dma((2 * n_exp,))] * 4
        + [dma((n_exp,))] * 2
        + [dma((2,))] * 2,
        compiler_params=pltpu.CompilerParams(
            collective_id=0, has_side_effects=True, vmem_limit_bytes=56 * 1024 * 1024
        ),
        cost_estimate=pl.CostEstimate(
            flops=4 * 8 * tok * width * hid,
            bytes_accessed=4 * width * hid,
            transcendentals=8 * tok * hid,
        ),
    )(tokens, gate_probs.T, expert_ids.T, priority[None, :], weight_in, weight_out)


def solution(mesh):
    placed = (
        P(("groups", "expert"), None),
        P(("groups", "expert"), None),
        P(("groups", "expert"), None),
        P(("groups", "expert")),
        P("expert", None, None),
        P("expert", None, None),
    )
    return jax.shard_map(
        shards, mesh=mesh, in_specs=placed, out_specs=P(("groups", "expert"), None), check_vma=False
    )
```

```python
import functools

import jax
import jax.numpy as jnp
from jax import lax
from jax.experimental import pallas as pl
from jax.experimental.pallas import tpu as pltpu
from jax.sharding import PartitionSpec as P

F32 = jnp.float32
BF16 = jnp.bfloat16


def gelu(x):
    return 0.5 * x * (1.0 + lax.erf(x * 0.7071067811865476))


def kernel(
    n_exp, base, tok, width,
    tokens, gates, ids, rank, w_in, w_out,
    out,
    w1, w2, snd, rows, xs, hs, ext_in, ext_out, give, got, keep, ysend, ygot, rsend, ret, info, acc,
    w_sem, z_s, z_r, fs_s, fs_r, fy_s, fy_r, ff_s, ff_r, g_s, g_r, y_s, y_r, r_s, r_r,
    mz_s, mz_r, mp_s, mp_r,
):
    tiles = width // 128
    tail = tiles * base
    cut = tail // 32 * 16
    halves = ((0, cut), (cut, tail + 16 - cut))
    me = lax.axis_index("expert")
    plane, col = me // 4, me % 4
    sibling = plane * 4 + (col // 2) * 2 + (col + 1) % 2
    across = plane * 4 + (col + 2) % 4

    def peer(j):
        return ((plane + j) % n_exp) * 4 + col

    def remote(src, dst, send, recv, dev):
        return pltpu.make_async_remote_copy(
            src_ref=src, dst_ref=dst, send_sem=send, recv_sem=recv,
            device_id={"expert": dev}, device_id_type=pl.DeviceIdType.MESH,
        )

    def dispatch(j):
        return remote(snd.at[j], rows.at[0, j], z_s.at[j], z_r.at[j], peer(n_exp - j))

    def to_sibling(d):
        return remote(rows.at[0, d], rows.at[1, d], fs_s.at[d], fs_r.at[d], sibling)

    def to_across(d):
        return remote(rows.at[0, d], rows.at[2, d], fy_s.at[d], fy_r.at[d], across)

    def pass_on(d):
        return remote(rows.at[2, d], rows.at[3, d], ff_s.at[d], ff_r.at[d], sibling)

    def give_copy(d):
        return remote(give.at[d], got.at[d], g_s.at[d], g_r.at[d], sibling)

    def pair_copy(d, h):
        span = pl.ds(*halves[h])
        return remote(
            ysend.at[d, span], ygot.at[d, span], y_s.at[2 * d + h], y_r.at[2 * d + h], across
        )

    def return_copy(d, h):
        span, j = pl.ds(*halves[h]), n_exp - d
        return remote(
            rsend.at[d, span], ret.at[j, span], r_s.at[2 * d + h], r_r.at[2 * j + h], peer(d)
        )

    def info_copy(j):
        return remote(info.at[0, 0], info.at[0, j], mz_s.at[j], mz_r.at[j], peer(n_exp - j))

    def info_sibling():
        return remote(info.at[0], info.at[1], mp_s.at[0], mp_r.at[0], sibling)

    def info_across():
        return remote(
            info.at[pl.ds(0, 2)], info.at[pl.ds(2, 2)], mp_s.at[1], mp_r.at[1], across
        )

    load_in = pltpu.make_async_copy(w_in.at[0], w1, w_sem.at[0])
    load_out = pltpu.make_async_copy(w_out.at[0], w2, w_sem.at[1])
    load_in.start()
    load_out.start()

    barrier = pltpu.get_barrier_semaphore()

    def greet(j, c):
        pl.semaphore_signal(
            barrier, inc=1, device_id={"expert": peer(j)}, device_id_type=pl.DeviceIdType.MESH
        )
        return c

    lax.fori_loop(1, n_exp, greet, 0)
    for dev in (sibling, across):
        pl.semaphore_signal(
            barrier, inc=1, device_id={"expert": dev}, device_id_type=pl.DeviceIdType.MESH
        )

    info[0, 0] = jnp.concatenate(
        [rank[...].astype(F32), ids[...].astype(F32), gates[...], jnp.zeros((3, tok), F32)], axis=0
    )
    ext_in[...] = jnp.zeros_like(ext_in)
    ext_out[...] = jnp.zeros_like(ext_out)
    first_row, second_row = ids[0:1, :], ids[1:2, :]
    upper = (
        lax.broadcasted_iota(jnp.int32, (tok, tok), 0)
        < lax.broadcasted_iota(jnp.int32, (tok, tok), 1)
    ).astype(BF16)
    slot_iota = lax.broadcasted_iota(jnp.int32, (base + 16, tok), 0).astype(F32)

    def pack(expert, dst):
        hit = ((first_row == expert) | (second_row == expert)).astype(F32)
        hit8 = jnp.broadcast_to(hit, (8, tok))
        place = jnp.dot(hit8.astype(BF16), upper, preferred_element_type=F32)[0:1, :]
        pick = jnp.where(slot_iota == place, hit, 0.0).astype(BF16)
        packed = jnp.dot(pick, tokens[...], preferred_element_type=F32)
        for c in range(tiles):
            lanes = slice(c * 128, (c + 1) * 128)
            dst[c * base : (c + 1) * base, :] = packed[:base, lanes].astype(BF16)
            ext_out[0, c : c + 1, :] = packed[base : base + 1, lanes]
        dst[tail : tail + 16, :] = ext_out[0].astype(BF16)

    pack(plane, rows.at[0, 0])
    pack((plane + n_exp - 1) % n_exp, snd.at[1])
    pl.semaphore_wait(barrier, n_exp + 1)
    to_across(0).start()
    to_sibling(0).start()

    def start_info(j, c):
        info_copy(j).start()
        return c

    lax.fori_loop(1, n_exp, start_info, 0)
    dispatch(1).start()

    def pack_send(j, c):
        pack((plane + n_exp - j) % n_exp, snd.at[j])
        return c

    lax.fori_loop(2, n_exp, pack_send, 0)

    def wait_info(j, c):
        info_copy(j).wait_recv()
        return c

    lax.fori_loop(1, n_exp, wait_info, 0)
    info_sibling().start()
    info_sibling().wait_recv()
    info_across().start()
    load_in.wait()
    load_out.wait()

    order = (1, 3, 0, 2)

    def finish(d, h):
        span = pl.ds(*halves[h])
        pair_copy(d, h).wait_recv()
        rsend[d, span] = (keep[d, 0, span] + ygot[d, span].astype(F32)).astype(BF16)

    def add_pair(d, h):
        span = pl.ds(*halves[h])
        ysend[d, span] = (keep[d, 1, span] + got[d, 1, span].astype(F32)).astype(BF16)
        pair_copy(d, h).start()

    def group(d, c):
        to_across(d).wait_recv()
        pass_on(d).start()

        @pl.when(d < n_exp - 1)
        def _():
            dispatch(d + 1).wait_send()

            @pl.when(d < n_exp - 2)
            def _():
                dispatch(d + 2).start()

            dispatch(d + 1).wait_recv()
            to_across(d + 1).start()
            to_sibling(d + 1).start()

        to_sibling(d).wait_recv()
        pass_on(d).wait_recv()
        for i, rel in enumerate(order):
            last = rows[rel, d, tail : tail + 16, :].astype(F32)
            for t in range(tiles):
                lanes = slice(t * 128, (t + 1) * 128)
                xs[i * base : (i + 1) * base, lanes] = rows[rel, d, t * base : (t + 1) * base, :]
                ext_in[i : i + 1, lanes] = last[t : t + 1, :]
        xs[4 * base :, :] = ext_in[...].astype(BF16)
        hid = w1.shape[1]
        for n in range(0, hid, 256):
            h = jnp.dot(xs[...], w1[:, n : n + 256], preferred_element_type=F32)
            hs[:, n : n + 256] = gelu(h).astype(BF16)
        for n in range(0, width, 256):
            wide = min(256, width - n)
            p = jnp.dot(hs[...], w2[:, n : n + wide], preferred_element_type=F32)
            for t in range(n // 128, (n + wide) // 128):
                q = p[:, t * 128 - n : (t + 1) * 128 - n]
                span = slice(t * base, (t + 1) * base)
                give[d, 0, span, :] = q[:base].astype(BF16)
                give[d, 1, span, :] = q[base : 2 * base].astype(BF16)
                keep[d, 0, span, :] = q[2 * base : 3 * base]
                keep[d, 1, span, :] = q[3 * base : 4 * base]
                for i in range(4):
                    ext_out[i, t : t + 1, :] = q[4 * base + i : 4 * base + i + 1]
        for i in range(2):
            give[d, i, tail : tail + 16, :] = ext_out[i].astype(BF16)
            keep[d, i, tail : tail + 16, :] = ext_out[2 + i]
        give_copy(d).start()

        @pl.when(d > 0)
        def _():
            finish(d - 1, 0)
            finish(d - 1, 1)

        @pl.when(d > 1)
        def _():
            return_copy(d - 1, 0).start()
            return_copy(d - 1, 1).start()

        give_copy(d).wait_recv()
        add_pair(d, 0)

        @pl.when(d < n_exp - 1)
        def _():
            add_pair(d, 1)

        keep[d, 0] = keep[d, 0] + got[d, 0].astype(F32)
        return c

    lax.fori_loop(0, n_exp, group, 0)

    info_across().wait_recv()
    own = jnp.transpose(jnp.concatenate([info[0, 0]] * (tok // 8), axis=0))
    mine, first, second = own[:, 0:1], own[:, 1:2], own[:, 2:3]

    def count(m, sums):
        r, k = m // n_exp, m % n_exp
        block = info[r, k]
        ahead = block[0:1, :] < mine
        one, two = block[1:2, :], block[2:3, :]
        a, b, c = sums
        a = a + jnp.where((one == first) & ahead, 1.0, 0.0)
        b = b + jnp.where(one == second, 1.0, 0.0)
        c = c + jnp.where((two == second) & ahead, 1.0, 0.0)
        return a, b, c

    zero = jnp.zeros((tok, tok), F32)
    sums = lax.fori_loop(0, 4 * n_exp, count, (zero, zero, zero))
    before_first, total_first, before_second = [jnp.sum(v, axis=1, keepdims=True) for v in sums]
    capacity = float(8 * tok)
    weight_first = jnp.where(before_first < capacity, own[:, 3:4], 0.0)
    weight_second = jnp.where(
        jnp.minimum(total_first, capacity) + before_second < capacity, own[:, 4:5], 0.0
    )
    lower = (
        lax.broadcasted_iota(jnp.int32, (tok, tok), 1)
        < lax.broadcasted_iota(jnp.int32, (tok, tok), 0)
    ).astype(BF16)
    lane = lax.broadcasted_iota(jnp.int32, (tok, tok), 1).astype(F32)

    def combine(expert, block):
        named = expert.astype(F32)
        one, two = first == named, second == named
        hit = jnp.where(one | two, 1.0, 0.0)
        weight = jnp.where(one, weight_first, jnp.where(two, weight_second, 0.0))
        place = jnp.dot(
            lower, jnp.broadcast_to(hit, (tok, tok)).astype(BF16), preferred_element_type=F32
        )
        pick = jnp.where(place == lane, hit, 0.0).astype(BF16)[:, :base]
        over = jnp.where(place[:, 0:1] == float(base), weight, 0.0) * hit
        last = block[tail : tail + 16, :].astype(F32)
        values = jnp.concatenate(
            [block[t * base : (t + 1) * base, :] for t in range(tiles)], axis=1
        )
        found = jnp.dot(pick, values, preferred_element_type=F32)
        for t in range(tiles):
            lanes = slice(t * 128, (t + 1) * 128)
            acc[:, lanes] += weight * found[:, lanes] + over * last[t : t + 1, :]

    acc[...] = jnp.zeros_like(acc)
    pair_copy(n_exp - 1, 0).wait_send()
    add_pair(n_exp - 1, 1)
    finish(n_exp - 1, 0)
    return_copy(n_exp - 1, 0).start()
    combine(plane, rsend.at[0])
    finish(n_exp - 1, 1)
    return_copy(n_exp - 1, 1).start()

    def collect(i, c):
        j = n_exp - i
        return_copy(i, 0).wait_recv()
        return_copy(i, 1).wait_recv()
        combine((plane + j) % n_exp, ret.at[j])
        return c

    lax.fori_loop(1, n_exp, collect, 0)
    out[...] = acc[...].astype(BF16)

    def drain(d, c):
        to_across(d).wait_send()
        to_sibling(d).wait_send()
        pass_on(d).wait_send()
        give_copy(d).wait_send()
        pair_copy(d, 1).wait_send()

        @pl.when(d < n_exp - 1)
        def _():
            pair_copy(d, 0).wait_send()

        @pl.when(d > 0)
        def _():
            info_copy(d).wait_send()
            return_copy(d, 0).wait_send()
            return_copy(d, 1).wait_send()

        return c

    lax.fori_loop(0, n_exp, drain, 0)
    info_sibling().wait_send()
    info_across().wait_send()


def shards(tokens, gate_probs, expert_ids, priority, weight_in, weight_out):
    tok, width = tokens.shape
    n_exp = lax.axis_size("expert") // 4
    base = 2 * tok // n_exp
    hid = weight_in.shape[2]
    block = (width // 128) * base + 16
    vmem = pl.BlockSpec(memory_space=pltpu.VMEM)
    hbm = pl.BlockSpec(memory_space=pl.ANY)
    group_rows = 4 * base + 16
    dma = pltpu.SemaphoreType.DMA
    return pl.pallas_call(
        functools.partial(kernel, n_exp, base, tok, width),
        out_shape=jax.ShapeDtypeStruct((tok, width), BF16),
        in_specs=[vmem, vmem, vmem, vmem, hbm, hbm],
        out_specs=vmem,
        scratch_shapes=[
            pltpu.VMEM((width, hid), BF16),
            pltpu.VMEM((hid, width), BF16),
            pltpu.VMEM((n_exp, block, 128), BF16),
            pltpu.VMEM((4, n_exp, block, 128), BF16),
            pltpu.VMEM((group_rows, width), BF16),
            pltpu.VMEM((group_rows, hid), BF16),
            pltpu.VMEM((16, width), F32),
            pltpu.VMEM((4, 16, 128), F32),
            pltpu.VMEM((n_exp, 2, block, 128), BF16),
            pltpu.VMEM((n_exp, 2, block, 128), BF16),
            pltpu.VMEM((n_exp, 2, block, 128), F32),
            pltpu.VMEM((n_exp, block, 128), BF16),
            pltpu.VMEM((n_exp, block, 128), BF16),
            pltpu.VMEM((n_exp, block, 128), BF16),
            pltpu.VMEM((n_exp, block, 128), BF16),
            pltpu.VMEM((4, n_exp, 8, tok), F32),
            pltpu.VMEM((tok, width), F32),
            dma((2,)),
        ]
        + [dma((n_exp,))] * 10
        + [dma((2 * n_exp,))] * 4
        + [dma((n_exp,))] * 2
        + [dma((2,))] * 2,
        compiler_params=pltpu.CompilerParams(
            collective_id=0, has_side_effects=True, vmem_limit_bytes=56 * 1024 * 1024
        ),
        cost_estimate=pl.CostEstimate(
            flops=4 * 8 * tok * width * hid,
            bytes_accessed=4 * width * hid,
            transcendentals=8 * tok * hid,
        ),
    )(tokens, gate_probs.T, expert_ids.T, priority[None, :], weight_in, weight_out)


def solution(mesh):
    placed = (
        P(("groups", "expert"), None),
        P(("groups", "expert"), None),
        P(("groups", "expert"), None),
        P(("groups", "expert")),
        P("expert", None, None),
        P("expert", None, None),
    )
    return jax.shard_map(
        shards, mesh=mesh, in_specs=placed, out_specs=P(("groups", "expert"), None), check_vma=False
    )
```
